32 devices in a mesh: ctx: 8 (over y, x, core), tp: 4 (over z).
Axes of the slice: x: 2, y: 2, z: 4, core: 2. Of those that a mesh axis runs over, the one named last changes fastest.
Arguments:
- queries: bfloat16 [2048, 8192], P('ctx', 'tp'), may hold values from -120 to 120
- key_proj: bfloat16 [2048, 1024], P('ctx', 'tp'), may hold values from -4 to 4
- value_proj: bfloat16 [2048, 1024], P('ctx', 'tp'), may hold values from -6 to 6
- out_weight: bfloat16 [8192, 8192], P('tp'), may hold values from -0.75 to 0.75
- doc_ids: int32 [2048], replicated, may hold values from 0 to 7, never falling along the last dimension, each value on 1 to 1024 neighbouring positions
- drop_seed: int32 [1], replicated, may hold values from 0 to 1073741823
Outputs:
- output: bfloat16 [2048, 8192], P('ctx', 'tp')
The draws below stay inside these ranges and needn't reach their ends.
Inputs may be any that keep to these rules, and one draw needn't show every extreme that they name: doc_ids never fall along the sequence; each document has 1 to 1024 tokens, one exactly 1024.
All inputs are finite; a program needn't handle non-finite values.
Results may differ from the reference program's by a relative error of at most 0.019.
Values may be sent and summed in bfloat16 or wider, within the bound.
A program may use at most 128 MiB of HBM per device.

```python
import math
import jax
import jax.numpy as jnp
import numpy as np
from jax import lax

D = 8192
HEADS = 64
KVH = 8
HD = 128
TOK_DEV = 256
DOCS = 8
SEQ = 2048


def shared_keys(key):
    drawn = jax.random.normal(jax.random.fold_in(key, 11), (SEQ, KVH * HD), jnp.float32)
    return jnp.clip(drawn, -4.0, 4.0)


def draw_key_proj(key, part):
    basis = shared_keys(key)
    return basis.astype(jnp.bfloat16)


def draw_queries(key, part):
    drawn = jax.random.normal(jax.random.fold_in(key, 13), (SEQ, HEADS * HD), jnp.float32)
    drawn = jnp.clip(drawn, -5.0, 5.0)
    return drawn.astype(jnp.bfloat16)


def block_scale(key, extent, cuts, low, largest):
    def one(axis_at, parts):
        steps = jax.random.uniform(jax.random.fold_in(jax.random.fold_in(key, 6), axis_at), (parts,), jnp.float32, low / len(cuts), largest / len(cuts))
        return jnp.repeat(jnp.exp(steps), extent[axis_at] // parts).reshape((-1,) + (1,) * (len(extent) - axis_at - 1))

    gain = one(*cuts[0])
    for cut in cuts[1:]:
        gain = gain * one(*cut)
    return gain


def length_profile(amount, total, bound, slope):
    weights = [(1 << 20) // math.isqrt(grade ** slope) + 1 for grade in range(2, amount + 1)]
    surplus, given = total - bound - (amount - 1), [1] * (amount - 1)
    while surplus > 0:
        movable = [i for i in range(amount - 1) if given[i] < bound]
        pool, left = sum([weights[i] for i in movable]), surplus
        for i in movable:
            extra = min(bound - given[i], max(1, left * weights[i] // pool), surplus)
            given[i] = given[i] + extra
            surplus = surplus - extra
    return np.array([bound] + given)


def ragged_sizes(key, number_of, total, most, lean):
    if number_of == 2:
        one = jax.random.randint(key, (), max(1, total - most), min(most, total - 1) + 1)
        return jnp.stack([one, total - one])
    tallies = jnp.asarray(length_profile(number_of, total, most, lean), jnp.int32)
    twos = (number_of - 1) // 2
    donor, receiver = tallies[1:1 + 2 * twos:2], tallies[2:2 + 2 * twos:2]
    room = jnp.minimum(donor - 1, most - receiver)
    shifted = jax.random.randint(jax.random.fold_in(key, 1), (twos,), 0, 1 << 20) % (room + 1)
    tallies = tallies.at[1:1 + 2 * twos:2].set(donor - shifted).at[2:2 + 2 * twos:2].set(receiver + shifted)
    return tallies[jax.random.permutation(jax.random.fold_in(key, 2), number_of)]


def gaussian(stream_key, dims, deviation, reach, pieces=(), kind=jnp.bfloat16):
    values = jax.random.normal(stream_key, dims, jnp.float32) * deviation
    if len(pieces) > 0:
        values = block_scale(stream_key, dims, pieces, -0.22, 0.18) * values
    return jnp.clip(values, min=-reach, max=reach).astype(kind)


def setup_inputs(seed: int = 0) -> dict:
    key_of = jax.random.split(jax.random.key(seed), 7)
    queries = draw_queries(jax.random.fold_in(key_of[6], 71), 0)
    key_proj = draw_key_proj(jax.random.fold_in(key_of[6], 71), 0)
    value_proj = gaussian(key_of[2], (SEQ, KVH * HD), 1.0, 6.0, ((0, 8), (1, 4)))
    out_weight = gaussian(key_of[3], (HEADS * HD, D), 64 ** -0.5, 0.75, ((0, 4),))
    doc_ids = jnp.searchsorted(jnp.cumsum(ragged_sizes(key_of[4], DOCS, SEQ, SEQ // 2, 0)), jnp.arange(SEQ), side="right").astype(jnp.int32)
    drop_seed = jax.random.randint(key_of[5], (1,), 0, 1073741824).astype(jnp.int32)
    return dict(queries=queries, key_proj=key_proj, value_proj=value_proj, out_weight=out_weight, doc_ids=doc_ids, drop_seed=drop_seed)


def mixing(value):
    value = value ^ lax.shift_right_logical(value, jnp.int32(16))
    value = value * 73244475
    value = value ^ lax.shift_right_logical(value, jnp.int32(16))
    value = value * 73244475
    value = value ^ lax.shift_right_logical(value, jnp.int32(16))
    return value


def reference(queries, key_proj, value_proj, out_weight, doc_ids, drop_seed):
    per_group = HEADS // KVH
    blocks = SEQ // TOK_DEV
    positions = jnp.arange(SEQ, dtype=jnp.int32)
    factor = HD ** -0.5

    def one_block(index):
        block = index // KVH
        group = index % KVH
        start = (block * TOK_DEV).astype(jnp.int32)
        column = (group * per_group * HD).astype(jnp.int32)
        q_rows = lax.dynamic_slice(queries, (start, column), (TOK_DEV, per_group * HD))
        q_rows = q_rows.reshape(TOK_DEV, per_group, HD).astype(jnp.float32)
        k_cols = lax.dynamic_slice_in_dim(key_proj, (group * HD).astype(jnp.int32), HD, 1).astype(jnp.float32)
        v_cols = lax.dynamic_slice_in_dim(value_proj, (group * HD).astype(jnp.int32), HD, 1).astype(jnp.float32)
        scores = jnp.einsum("qgd,nd->qgn", q_rows, k_cols) * factor
        q_pos = start + jnp.arange(TOK_DEV, dtype=jnp.int32)
        q_doc = lax.dynamic_slice_in_dim(doc_ids, start, TOK_DEV)
        allowed = (q_doc[:, None] == doc_ids[None, :]) & (positions[None, :] <= q_pos[:, None])
        allowed = allowed[:, None, :]
        peak = jnp.max(jnp.where(allowed, scores, jnp.float32(-1e30)), axis=-1)
        weights = jnp.where(allowed, jnp.exp(scores - peak[..., None]), jnp.float32(0.0))
        row_sum = jnp.sum(weights, axis=-1)
        head_ids = (group * per_group + jnp.arange(per_group, dtype=jnp.int32)).reshape(1, per_group, 1)
        q_hash = mixing(mixing(drop_seed[0] * 7919 + head_ids) ^ (q_pos.reshape(TOK_DEV, 1, 1) * 65537))
        full_hash = mixing(q_hash + positions.reshape(1, 1, SEQ))
        keeper = lax.shift_right_logical(full_hash, jnp.int32(8)) >= 1677722
        dropped = jnp.where(keeper, weights * jnp.float32(1.0 / 0.9), jnp.float32(0.0)).astype(jnp.bfloat16)
        mixed = jnp.einsum("qgn,nd->qgd", dropped.astype(jnp.float32), v_cols) / row_sum[..., None]
        return mixed.astype(jnp.bfloat16)

    results = lax.map(one_block, jnp.arange(blocks * KVH, dtype=jnp.int32))
    attention = results.reshape(blocks, KVH, TOK_DEV, per_group, HD)
    attention = attention.transpose(0, 2, 1, 3, 4).reshape(SEQ, HEADS * HD)
    return jnp.dot(attention, out_weight, preferred_element_type=jnp.float32).astype(jnp.bfloat16)
```

```python
import functools

import jax
import jax.numpy as jnp
from jax import lax
from jax.experimental import pallas as pl
from jax.experimental.pallas import tpu as pltpu
from jax.sharding import PartitionSpec as P

HEADS = 64
KVH = 8
HD = 128
PAIR = 2
EXP2_SCALE = HD ** (-0.5) * 1.4426950408889634


def half_mixing(value):
    value = value ^ lax.shift_right_logical(value, jnp.int32(16))
    value = value * 73244475
    value = value ^ lax.shift_right_logical(value, jnp.int32(16))
    return value * 73244475


def mixing(value):
    value = half_mixing(value)
    return value ^ lax.shift_right_logical(value, jnp.int32(16))


def attend_kernel(meta_ref, q_ref, kv_ref, start_ref, out_ref):
    rows = q_ref.shape[0]
    pair = q_ref.shape[1] // HD
    step = pl.program_id(0)
    first_tile, block, seed, head_base = meta_ref[0], meta_ref[1], meta_ref[2], meta_ref[3]
    group = (step * pair) // (HEADS // KVH)
    q_pos = block * rows + lax.broadcasted_iota(jnp.int32, (1, rows), 1)
    doc_start = start_ref[...]
    k_iota = lax.broadcasted_iota(jnp.int32, (rows, rows), 0)
    hashes = []
    for n in range(pair):
        head = jnp.full((1, rows), head_base + step * pair + n, jnp.int32)
        hashes.append(mixing(mixing(seed * 7919 + head) ^ (q_pos * 65537)))

    def tile(number, state, diagonal):
        base = number * rows
        k_tile = kv_ref[number, group, 0:rows, :]
        v_tile = jnp.concatenate(
            [kv_ref[number, group, rows + HD * m : rows + HD * (m + 1), :] for m in range(rows // HD)],
            axis=1,
        )
        allowed = k_iota >= doc_start - base
        if diagonal:
            allowed = allowed & (k_iota <= q_pos - base)
        result = []
        for n in range(pair):
            q_head = q_ref[:, n * HD : (n + 1) * HD]
            scores = lax.dot_general(
                k_tile, q_head, (((1,), (1,)), ((), ())), preferred_element_type=jnp.float32
            )
            scores = jnp.where(allowed, scores, jnp.float32(-1e30))
            tile_max = jnp.max(scores, axis=0, keepdims=True)
            peak = tile_max if diagonal else jnp.maximum(state[n][0], tile_max)
            weights = jnp.exp2((scores - peak) * EXP2_SCALE)
            total = jnp.sum(weights, axis=0, keepdims=True)
            mixed = mixing((hashes[n] + base) + k_iota)
            keeper = lax.shift_right_logical(mixed, jnp.int32(8)) >= 1677722
            dropped = jnp.where(keeper, weights, jnp.float32(0.0)).astype(jnp.bfloat16)
            value = jnp.dot(v_tile, dropped, preferred_element_type=jnp.float32)
            if not diagonal:
                rescale = jnp.exp2((state[n][0] - peak) * EXP2_SCALE)
                total = state[n][1] * rescale + total
                value = state[n][2] * rescale + value
            result.append((peak, total, value))
        return tuple(result)

    state = tile(block, None, True)
    state = lax.fori_loop(first_tile, block, lambda i, s: tile(i, s, False), state)
    for n in range(pair):
        _, total, value = state[n]
        value = value * (jnp.float32(1.0 / 0.9) / total)
        out_ref[:, n * HD : (n + 1) * HD] = value.T.astype(jnp.bfloat16)


def attend(queries, kv_all, doc_ids, drop_seed):
    rows, width = queries.shape
    local_heads = width // HD
    ctx_index = lax.axis_index("ctx").astype(jnp.int32)
    tp_index = lax.axis_index("tp").astype(jnp.int32)
    q_doc = lax.dynamic_slice_in_dim(doc_ids, ctx_index * rows, rows)
    doc_start = jnp.sum((doc_ids[:, None] < q_doc[None, :]).astype(jnp.int32), axis=0)
    meta = jnp.stack([doc_start[0] // rows, ctx_index, drop_seed[0], tp_index * local_heads])
    return pl.pallas_call(
        attend_kernel,
        grid_spec=pltpu.PrefetchScalarGridSpec(
            num_scalar_prefetch=1,
            grid=(local_heads // PAIR,),
            in_specs=[
                pl.BlockSpec((rows, PAIR * HD), lambda i, m: (0, i)),
                pl.BlockSpec(kv_all.shape, lambda i, m: (0, 0, 0, 0)),
                pl.BlockSpec((1, rows), lambda i, m: (0, 0)),
            ],
            out_specs=pl.BlockSpec((rows, PAIR * HD), lambda i, m: (0, i)),
        ),
        out_shape=jax.ShapeDtypeStruct(queries.shape, jnp.bfloat16),
        compiler_params=pltpu.CompilerParams(vmem_limit_bytes=48 * 1024 * 1024),
    )(meta, queries, kv_all, doc_start.reshape(1, rows))


def pack_kv(key_proj, value_proj):
    rows = key_proj.shape[0]
    local_kv = key_proj.shape[1] // HD
    keys = key_proj.reshape(rows, local_kv, HD).transpose(1, 0, 2)
    values = value_proj.reshape(rows // HD, HD, local_kv, HD).transpose(2, 0, 3, 1)
    return jnp.concatenate([keys, values.reshape(local_kv, rows, HD)], axis=1)


def body(queries, key_proj, value_proj, out_weight, doc_ids, drop_seed):
    kv_all = lax.all_gather(pack_kv(key_proj, value_proj), "ctx", axis=0)
    attention = attend(queries, kv_all, doc_ids, drop_seed)
    partial_value = jnp.dot(attention, out_weight, preferred_element_type=jnp.float32)
    return lax.psum_scatter(
        partial_value.astype(jnp.bfloat16), "tp", scatter_dimension=1, tiled=True
    )


def solution(mesh):
    in_specs = (P("ctx", "tp"), P("ctx", "tp"), P("ctx", "tp"), P("tp", None), P(), P())
    out_specs = P("ctx", "tp")
    return jax.shard_map(body, mesh=mesh, in_specs=in_specs, out_specs=out_specs, check_vma=False)
```

```python
import functools

import jax
import jax.numpy as jnp
from jax import lax
from jax.experimental import pallas as pl
from jax.experimental.pallas import tpu as pltpu
from jax.sharding import PartitionSpec as P

HEADS = 64
KVH = 8
HD = 128
PAIR = 2
EXP2_SCALE = HD ** (-0.5) * 1.4426950408889634


def half_mixing(value):
    value = value ^ lax.shift_right_logical(value, jnp.int32(16))
    value = value * 73244475
    value = value ^ lax.shift_right_logical(value, jnp.int32(16))
    return value * 73244475


def mixing(value):
    value = half_mixing(value)
    return value ^ lax.shift_right_logical(value, jnp.int32(16))


def attend_kernel(meta_ref, q_ref, kv_ref, start_ref, out_ref):
    rows = q_ref.shape[0]
    pair = q_ref.shape[1] // HD
    step = pl.program_id(0)
    first_tile, block, seed, head_base = meta_ref[0], meta_ref[1], meta_ref[2], meta_ref[3]
    group = (step * pair) // (HEADS // KVH)
    q_pos = block * rows + lax.broadcasted_iota(jnp.int32, (1, rows), 1)
    doc_start = start_ref[...]
    k_iota = lax.broadcasted_iota(jnp.int32, (rows, rows), 0)
    hashes = []
    for n in range(pair):
        head = jnp.full((1, rows), head_base + step * pair + n, jnp.int32)
        hashes.append(mixing(mixing(seed * 7919 + head) ^ (q_pos * 65537)))

    def tile(number, state, diagonal):
        base = number * rows
        k_tile = kv_ref[number, group, 0:rows, :]
        v_tile = jnp.concatenate(
            [kv_ref[number, group, rows + HD * m : rows + HD * (m + 1), :] for m in range(rows // HD)],
            axis=1,
        )
        allowed = k_iota >= doc_start - base
        if diagonal:
            allowed = allowed & (k_iota <= q_pos - base)
        result = []
        for n in range(pair):
            q_head = q_ref[:, n * HD : (n + 1) * HD]
            scores = lax.dot_general(
                k_tile, q_head, (((1,), (1,)), ((), ())), preferred_element_type=jnp.float32
            )
            scores = jnp.where(allowed, scores, jnp.float32(-1e30))
            tile_max = jnp.max(scores, axis=0, keepdims=True)
            peak = tile_max if diagonal else jnp.maximum(state[n][0], tile_max)
            weights = jnp.exp2((scores - peak) * EXP2_SCALE)
            total = jnp.sum(weights, axis=0, keepdims=True)
            mixed = mixing((hashes[n] + base) + k_iota)
            keeper = lax.shift_right_logical(mixed, jnp.int32(8)) >= 1677722
            dropped = jnp.where(keeper, weights, jnp.float32(0.0)).astype(jnp.bfloat16)
            value = jnp.dot(v_tile, dropped, preferred_element_type=jnp.float32)
            if not diagonal:
                rescale = jnp.exp2((state[n][0] - peak) * EXP2_SCALE)
                total = state[n][1] * rescale + total
                value = state[n][2] * rescale + value
            result.append((peak, total, value))
        return tuple(result)

    state = tile(block, None, True)
    state = lax.fori_loop(first_tile, block, lambda i, s: tile(i, s, False), state)
    for n in range(pair):
        _, total, value = state[n]
        value = value * (jnp.float32(1.0 / 0.9) / total)
        out_ref[:, n * HD : (n + 1) * HD] = value.T.astype(jnp.bfloat16)


def attend(queries, kv_all, doc_ids, drop_seed):
    rows, width = queries.shape
    local_heads = width // HD
    ctx_index = lax.axis_index("ctx").astype(jnp.int32)
    tp_index = lax.axis_index("tp").astype(jnp.int32)
    q_doc = lax.dynamic_slice_in_dim(doc_ids, ctx_index * rows, rows)
    doc_start = jnp.sum((doc_ids[:, None] < q_doc[None, :]).astype(jnp.int32), axis=0)
    meta = jnp.stack([doc_start[0] // rows, ctx_index, drop_seed[0], tp_index * local_heads])
    return pl.pallas_call(
        attend_kernel,
        grid_spec=pltpu.PrefetchScalarGridSpec(
            num_scalar_prefetch=1,
            grid=(local_heads // PAIR,),
            in_specs=[
                pl.BlockSpec((rows, PAIR * HD), lambda i, m: (0, i)),
                pl.BlockSpec(kv_all.shape, lambda i, m: (0, 0, 0, 0)),
                pl.BlockSpec((1, rows), lambda i, m: (0, 0)),
            ],
            out_specs=pl.BlockSpec((rows, PAIR * HD), lambda i, m: (0, i)),
        ),
        out_shape=jax.ShapeDtypeStruct(queries.shape, jnp.bfloat16),
        compiler_params=pltpu.CompilerParams(vmem_limit_bytes=48 * 1024 * 1024),
    )(meta, queries, kv_all, doc_start.reshape(1, rows))


def pack_kv(key_proj, value_proj):
    rows = key_proj.shape[0]
    local_kv = key_proj.shape[1] // HD
    keys = key_proj.reshape(rows, local_kv, HD).transpose(1, 0, 2)
    values = value_proj.reshape(rows // HD, HD, local_kv, HD).transpose(2, 0, 3, 1)
    return jnp.concatenate([keys, values.reshape(local_kv, rows, HD)], axis=1)


def project_kernel(size, subs, att_ref, weight_ref, out_ref, own, from_left, from_right, w_buf, w_sem, send_r, recv_r, send_l, recv_l):
    me = lax.axis_index("tp")
    width = w_buf.shape[2]
    tiles = size * subs
    slots = w_buf.shape[0]
    upper = (2 * me) // size

    def target(i):
        k = i // subs
        a = (k // 2) * (1 - k % 2) + (size - 1 - k // 2) * (k % 2)
        return a * upper + (size - 1 - a) * (1 - upper)

    def weight_copy(i):
        column = pl.multiple_of((target(i) * subs + i % subs) * width, width)
        return pltpu.make_async_copy(
            weight_ref.at[:, pl.ds(column, width)], w_buf.at[i % slots], w_sem.at[i % slots]
        )

    def right_copy(t, s):
        return pltpu.make_async_remote_copy(
            src_ref=own.at[t, s], dst_ref=from_left.at[t, s], send_sem=send_r.at[t, s],
            recv_sem=recv_r.at[t, s], device_id={"tp": lax.rem(me + 1, size)},
            device_id_type=pl.DeviceIdType.MESH,
        )

    def left_copy(t, s):
        return pltpu.make_async_remote_copy(
            src_ref=own.at[t, s], dst_ref=from_right.at[t, s], send_sem=send_l.at[t, s],
            recv_sem=recv_l.at[t, s], device_id={"tp": lax.rem(me + size - 1, size)},
            device_id_type=pl.DeviceIdType.MESH,
        )

    for i in range(slots - 1):
        weight_copy(i).start()
    barrier = pltpu.get_barrier_semaphore()

    @pl.when(me > 0)
    def _():
        pl.semaphore_signal(barrier, inc=1, device_id={"tp": me - 1}, device_id_type=pl.DeviceIdType.MESH)

    @pl.when(me < size - 1)
    def _():
        pl.semaphore_signal(barrier, inc=1, device_id={"tp": me + 1}, device_id_type=pl.DeviceIdType.MESH)

    @pl.when((me > 0) & (me < size - 1))
    def _():
        pl.semaphore_wait(barrier, 2)

    @pl.when((me == 0) | (me == size - 1))
    def _():
        pl.semaphore_wait(barrier, 1)

    def make_tile(i, carry):
        @pl.when(i + slots - 1 < tiles)
        def _():
            weight_copy(i + slots - 1).start()

        weight_copy(i).wait()
        t, s = target(i), i % subs
        own[t, s] = jnp.dot(
            att_ref[...], w_buf[i % slots], preferred_element_type=jnp.float32
        ).astype(jnp.bfloat16)

        @pl.when((me == 0) & (t > 0))
        def _():
            right_copy(t, s).start()

        @pl.when((me == size - 1) & (t < size - 1))
        def _():
            left_copy(t, s).start()

        return carry

    lax.fori_loop(0, tiles, make_tile, 0)

    def add(ref, t, s):
        total = own[t, s].astype(jnp.float32) + ref[t, s].astype(jnp.float32)
        own[t, s] = total.astype(jnp.bfloat16)

    def hand_on(i, carry):
        s = i % subs
        right_t = size - 1 - i // subs
        left_t = i // subs

        @pl.when((me > 0) & (right_t > me))
        def _():
            right_copy(right_t, s).wait_recv()
            add(from_left, right_t, s)
            right_copy(right_t, s).start()

        @pl.when((me < size - 1) & (left_t < me))
        def _():
            left_copy(left_t, s).wait_recv()
            add(from_right, left_t, s)
            left_copy(left_t, s).start()

        return carry

    lax.fori_loop(0, tiles, hand_on, 0)

    for s in range(subs):
        columns = slice(s * width, (s + 1) * width)

        @pl.when(me == 0)
        def _():
            left_copy(me, s).wait_recv()
            out_ref[:, columns] = (
                own[me, s].astype(jnp.float32) + from_right[me, s].astype(jnp.float32)
            ).astype(jnp.bfloat16)

        @pl.when(me == size - 1)
        def _():
            right_copy(me, s).wait_recv()
            out_ref[:, columns] = (
                own[me, s].astype(jnp.float32) + from_left[me, s].astype(jnp.float32)
            ).astype(jnp.bfloat16)

        @pl.when((me > 0) & (me < size - 1))
        def _():
            right_copy(me, s).wait_recv()
            left_copy(me, s).wait_recv()
            out_ref[:, columns] = (
                own[me, s].astype(jnp.float32)
                + from_left[me, s].astype(jnp.float32)
                + from_right[me, s].astype(jnp.float32)
            ).astype(jnp.bfloat16)

    def drain(i, carry):
        t, s = i // subs, i % subs

        @pl.when(t > me)
        def _():
            right_copy(t, s).wait_send()

        @pl.when(t < me)
        def _():
            left_copy(t, s).wait_send()

        return carry

    lax.fori_loop(0, tiles, drain, 0)


def project(attention, out_weight, size):
    rows, features = attention.shape
    columns = out_weight.shape[1] // size
    width = min(512, columns)
    subs = columns // width
    block = pltpu.VMEM((size, subs, rows, width), jnp.bfloat16)
    sems = pltpu.SemaphoreType.DMA((size, subs))
    return pl.pallas_call(
        functools.partial(project_kernel, size, subs),
        out_shape=jax.ShapeDtypeStruct((rows, columns), jnp.bfloat16),
        in_specs=[pl.BlockSpec(memory_space=pltpu.VMEM), pl.BlockSpec(memory_space=pl.ANY)],
        out_specs=pl.BlockSpec(memory_space=pltpu.VMEM),
        scratch_shapes=[
            block, block, block,
            pltpu.VMEM((3, features, width), jnp.bfloat16),
            pltpu.SemaphoreType.DMA((3,)),
            sems, sems, sems, sems,
        ],
        compiler_params=pltpu.CompilerParams(
            collective_id=0, has_side_effects=True, vmem_limit_bytes=48 * 1024 * 1024
        ),
    )(attention, out_weight)


def body(size, queries, key_proj, value_proj, out_weight, doc_ids, drop_seed):
    kv_all = lax.all_gather(pack_kv(key_proj, value_proj), "ctx", axis=0)
    attention = attend(queries, kv_all, doc_ids, drop_seed)
    return project(attention, out_weight, size)


def solution(mesh):
    in_specs = (P("ctx", "tp"), P("ctx", "tp"), P("ctx", "tp"), P("tp", None), P(), P())
    out_specs = P("ctx", "tp")
    return jax.shard_map(
        functools.partial(body, mesh.shape["tp"]), mesh=mesh, in_specs=in_specs, out_specs=out_specs, check_vma=False
    )
```

```python
import functools

import jax
import jax.numpy as jnp
from jax import lax
from jax.experimental import pallas as pl
from jax.experimental.pallas import tpu as pltpu
from jax.sharding import PartitionSpec as P

HEADS = 64
KVH = 8
HD = 128
PAIR = 2
EXP2_SCALE = HD ** (-0.5) * 1.4426950408889634


def half_mixing(value):
    value = value ^ lax.shift_right_logical(value, jnp.int32(16))
    value = value * 73244475
    value = value ^ lax.shift_right_logical(value, jnp.int32(16))
    return value * 73244475


def mixing(value):
    value = half_mixing(value)
    return value ^ lax.shift_right_logical(value, jnp.int32(16))


def attend_kernel(meta_ref, q_ref, kv_ref, start_ref, out_ref):
    rows = q_ref.shape[0]
    pair = q_ref.shape[1] // HD
    step = pl.program_id(0)
    first_tile, block, seed, head_base = meta_ref[0], meta_ref[1], meta_ref[2], meta_ref[3]
    group = (step * pair) // (HEADS // KVH)
    q_pos = block * rows + lax.broadcasted_iota(jnp.int32, (1, rows), 1)
    doc_start = start_ref[...]
    k_iota = lax.broadcasted_iota(jnp.int32, (rows, rows), 0)
    hashes = []
    for n in range(pair):
        head = jnp.full((1, rows), head_base + step * pair + n, jnp.int32)
        hashes.append(mixing(mixing(seed * 7919 + head) ^ (q_pos * 65537)))

    def tile(number, state, diagonal):
        base = number * rows
        k_tile = kv_ref[number, group, 0:rows, :]
        v_tile = jnp.concatenate(
            [kv_ref[number, group, rows + HD * m : rows + HD * (m + 1), :] for m in range(rows // HD)],
            axis=1,
        )
        allowed = k_iota >= doc_start - base
        if diagonal:
            allowed = allowed & (k_iota <= q_pos - base)
        result = []
        for n in range(pair):
            q_head = q_ref[:, n * HD : (n + 1) * HD]
            scores = lax.dot_general(
                k_tile, q_head, (((1,), (1,)), ((), ())), preferred_element_type=jnp.float32
            )
            scores = jnp.where(allowed, scores, jnp.float32(-1e30))
            tile_max = jnp.max(scores, axis=0, keepdims=True)
            peak = tile_max if diagonal else jnp.maximum(state[n][0], tile_max)
            weights = jnp.exp2((scores - peak) * EXP2_SCALE)
            total = jnp.sum(weights, axis=0, keepdims=True)
            mixed = mixing((hashes[n] + base) + k_iota)
            keeper = lax.shift_right_logical(mixed, jnp.int32(8)) >= 1677722
            dropped = jnp.where(keeper, weights, jnp.float32(0.0)).astype(jnp.bfloat16)
            value = jnp.dot(v_tile, dropped, preferred_element_type=jnp.float32)
            if not diagonal:
                rescale = jnp.exp2((state[n][0] - peak) * EXP2_SCALE)
                total = state[n][1] * rescale + total
                value = state[n][2] * rescale + value
            result.append((peak, total, value))
        return tuple(result)

    state = tile(block, None, True)
    state = lax.fori_loop(first_tile, block, lambda i, s: tile(i, s, False), state)
    for n in range(pair):
        _, total, value = state[n]
        value = value * (jnp.float32(1.0 / 0.9) / total)
        out_ref[:, n * HD : (n + 1) * HD] = value.T.astype(jnp.bfloat16)


def attend(queries, kv_all, doc_ids, drop_seed):
    rows, width = queries.shape
    local_heads = width // HD
    ctx_index = lax.axis_index("ctx").astype(jnp.int32)
    tp_index = lax.axis_index("tp").astype(jnp.int32)
    q_doc = lax.dynamic_slice_in_dim(doc_ids, ctx_index * rows, rows)
    doc_start = jnp.sum((doc_ids[:, None] < q_doc[None, :]).astype(jnp.int32), axis=0)
    meta = jnp.stack([doc_start[0] // rows, ctx_index, drop_seed[0], tp_index * local_heads])
    return pl.pallas_call(
        attend_kernel,
        grid_spec=pltpu.PrefetchScalarGridSpec(
            num_scalar_prefetch=1,
            grid=(local_heads // PAIR,),
            in_specs=[
                pl.BlockSpec((rows, PAIR * HD), lambda i, m: (0, i)),
                pl.BlockSpec(kv_all.shape, lambda i, m: (0, 0, 0, 0)),
                pl.BlockSpec((1, rows), lambda i, m: (0, 0)),
            ],
            out_specs=pl.BlockSpec((rows, PAIR * HD), lambda i, m: (0, i)),
        ),
        out_shape=jax.ShapeDtypeStruct(queries.shape, jnp.bfloat16),
        compiler_params=pltpu.CompilerParams(vmem_limit_bytes=48 * 1024 * 1024),
    )(meta, queries, kv_all, doc_start.reshape(1, rows))


def pack_kv(key_proj, value_proj):
    rows = key_proj.shape[0]
    local_kv = key_proj.shape[1] // HD
    keys = key_proj.reshape(rows, local_kv, HD).transpose(1, 0, 2)
    values = value_proj.reshape(rows // HD, HD, local_kv, HD).transpose(2, 0, 3, 1)
    return jnp.concatenate([keys, values.reshape(local_kv, rows, HD)], axis=1)


def project_kernel(size, subs, att_ref, weight_ref, out_ref, own, from_left, from_right, w_buf, w_sem, send_r, recv_r, send_l, recv_l):
    me = lax.axis_index("tp")
    width = w_buf.shape[2]
    tiles = size * subs
    slots = w_buf.shape[0]
    upper = (2 * me) // size

    def target(i):
        k = i // subs
        a = (k // 2) * (1 - k % 2) + (size - 1 - k // 2) * (k % 2)
        return a * upper + (size - 1 - a) * (1 - upper)

    def weight_copy(i):
        column = pl.multiple_of((target(i) * subs + i % subs) * width, width)
        return pltpu.make_async_copy(
            weight_ref.at[:, pl.ds(column, width)], w_buf.at[i % slots], w_sem.at[i % slots]
        )

    def right_copy(t, s):
        return pltpu.make_async_remote_copy(
            src_ref=own.at[t, s], dst_ref=from_left.at[t, s], send_sem=send_r.at[t, s],
            recv_sem=recv_r.at[t, s], device_id={"tp": lax.rem(me + 1, size)},
            device_id_type=pl.DeviceIdType.MESH,
        )

    def left_copy(t, s):
        return pltpu.make_async_remote_copy(
            src_ref=own.at[t, s], dst_ref=from_right.at[t, s], send_sem=send_l.at[t, s],
            recv_sem=recv_l.at[t, s], device_id={"tp": lax.rem(me + size - 1, size)},
            device_id_type=pl.DeviceIdType.MESH,
        )

    for i in range(slots - 1):
        weight_copy(i).start()
    barrier = pltpu.get_barrier_semaphore()

    @pl.when(me > 0)
    def _():
        pl.semaphore_signal(barrier, inc=1, device_id={"tp": me - 1}, device_id_type=pl.DeviceIdType.MESH)

    @pl.when(me < size - 1)
    def _():
        pl.semaphore_signal(barrier, inc=1, device_id={"tp": me + 1}, device_id_type=pl.DeviceIdType.MESH)

    @pl.when((me > 0) & (me < size - 1))
    def _():
        pl.semaphore_wait(barrier, 2)

    @pl.when((me == 0) | (me == size - 1))
    def _():
        pl.semaphore_wait(barrier, 1)

    def make_tile(i, carry):
        @pl.when(i + slots - 1 < tiles)
        def _():
            weight_copy(i + slots - 1).start()

        weight_copy(i).wait()
        t, s = target(i), i % subs
        own[t, s] = jnp.dot(
            att_ref[...], w_buf[i % slots], preferred_element_type=jnp.float32
        ).astype(jnp.bfloat16)

        @pl.when((me == 0) & (t > 0))
        def _():
            right_copy(t, s).start()

        @pl.when((me == size - 1) & (t < size - 1))
        def _():
            left_copy(t, s).start()

        return carry

    lax.fori_loop(0, tiles, make_tile, 0)

    def add(ref, t, s):
        total = own[t, s].astype(jnp.float32) + ref[t, s].astype(jnp.float32)
        own[t, s] = total.astype(jnp.bfloat16)

    def hand_on(i, carry):
        s = i % subs
        right_t = size - 1 - i // subs
        left_t = i // subs

        @pl.when((me > 0) & (right_t > me))
        def _():
            right_copy(right_t, s).wait_recv()
            add(from_left, right_t, s)
            right_copy(right_t, s).start()

        @pl.when((me < size - 1) & (left_t < me))
        def _():
            left_copy(left_t, s).wait_recv()
            add(from_right, left_t, s)
            left_copy(left_t, s).start()

        return carry

    lax.fori_loop(0, tiles, hand_on, 0)

    for s in range(subs):
        columns = slice(s * width, (s + 1) * width)

        @pl.when(me == 0)
        def _():
            left_copy(me, s).wait_recv()
            out_ref[:, columns] = (
                own[me, s].astype(jnp.float32) + from_right[me, s].astype(jnp.float32)
            ).astype(jnp.bfloat16)

        @pl.when(me == size - 1)
        def _():
            right_copy(me, s).wait_recv()
            out_ref[:, columns] = (
                own[me, s].astype(jnp.float32) + from_left[me, s].astype(jnp.float32)
            ).astype(jnp.bfloat16)

        @pl.when((me > 0) & (me < size - 1))
        def _():
            right_copy(me, s).wait_recv()
            left_copy(me, s).wait_recv()
            out_ref[:, columns] = (
                own[me, s].astype(jnp.float32)
                + from_left[me, s].astype(jnp.float32)
                + from_right[me, s].astype(jnp.float32)
            ).astype(jnp.bfloat16)

    def drain(i, carry):
        t, s = i // subs, i % subs

        @pl.when(t > me)
        def _():
            right_copy(t, s).wait_send()

        @pl.when(t < me)
        def _():
            left_copy(t, s).wait_send()

        return carry

    lax.fori_loop(0, tiles, drain, 0)


def project(attention, out_weight, size):
    rows, features = attention.shape
    columns = out_weight.shape[1] // size
    width = min(256, columns)
    subs = columns // width
    block = pltpu.VMEM((size, subs, rows, width), jnp.bfloat16)
    sems = pltpu.SemaphoreType.DMA((size, subs))
    return pl.pallas_call(
        functools.partial(project_kernel, size, subs),
        out_shape=jax.ShapeDtypeStruct((rows, columns), jnp.bfloat16),
        in_specs=[pl.BlockSpec(memory_space=pltpu.VMEM), pl.BlockSpec(memory_space=pl.ANY)],
        out_specs=pl.BlockSpec(memory_space=pltpu.VMEM),
        scratch_shapes=[
            block, block, block,
            pltpu.VMEM((3, features, width), jnp.bfloat16),
            pltpu.SemaphoreType.DMA((3,)),
            sems, sems, sems, sems,
        ],
        compiler_params=pltpu.CompilerParams(
            collective_id=0, has_side_effects=True, vmem_limit_bytes=48 * 1024 * 1024
        ),
    )(attention, out_weight)


def body(size, queries, key_proj, value_proj, out_weight, doc_ids, drop_seed):
    kv_all = lax.all_gather(pack_kv(key_proj, value_proj), "ctx", axis=0)
    attention = attend(queries, kv_all, doc_ids, drop_seed)
    return project(attention, out_weight, size)


def solution(mesh):
    in_specs = (P("ctx", "tp"), P("ctx", "tp"), P("ctx", "tp"), P("tp", None), P(), P())
    out_specs = P("ctx", "tp")
    return jax.shard_map(
        functools.partial(body, mesh.shape["tp"]), mesh=mesh, in_specs=in_specs, out_specs=out_specs, check_vma=False
    )
```

```python
import functools

import jax
import jax.numpy as jnp
from jax import lax
from jax.experimental import pallas as pl
from jax.experimental.pallas import tpu as pltpu
from jax.sharding import PartitionSpec as P

HEADS = 64
KVH = 8
HD = 128
PAIR = 4
EXP2_SCALE = HD ** (-0.5) * 1.4426950408889634


def half_mixing(value):
    value = value ^ lax.shift_right_logical(value, jnp.int32(16))
    value = value * 73244475
    value = value ^ lax.shift_right_logical(value, jnp.int32(16))
    return value * 73244475


def mixing(value):
    value = half_mixing(value)
    return value ^ lax.shift_right_logical(value, jnp.int32(16))


def attend_kernel(meta_ref, q_ref, kv_ref, start_ref, out_ref):
    rows = q_ref.shape[0]
    pair = q_ref.shape[1] // HD
    step = pl.program_id(0)
    first_tile, block, seed, head_base = meta_ref[0], meta_ref[1], meta_ref[2], meta_ref[3]
    group = (step * pair) // (HEADS // KVH)
    q_pos = block * rows + lax.broadcasted_iota(jnp.int32, (1, rows), 1)
    doc_start = start_ref[...]
    k_iota = lax.broadcasted_iota(jnp.int32, (rows, rows), 0)
    hashes = []
    for n in range(pair):
        head = jnp.full((1, rows), head_base + step * pair + n, jnp.int32)
        hashes.append(mixing(mixing(seed * 7919 + head) ^ (q_pos * 65537)))

    def tile(number, state, diagonal):
        base = number * rows
        k_tile = kv_ref[number, group, 0:rows, :]
        v_tile = jnp.concatenate(
            [kv_ref[number, group, rows + HD * m : rows + HD * (m + 1), :] for m in range(rows // HD)],
            axis=1,
        )
        allowed = k_iota >= doc_start - base
        if diagonal:
            allowed = allowed & (k_iota <= q_pos - base)
        result = []
        for n in range(pair):
            q_head = q_ref[:, n * HD : (n + 1) * HD]
            scores = lax.dot_general(
                k_tile, q_head, (((1,), (1,)), ((), ())), preferred_element_type=jnp.float32
            )
            scores = jnp.where(allowed, scores, jnp.float32(-1e30))
            tile_max = jnp.max(scores, axis=0, keepdims=True)
            peak = tile_max if diagonal else jnp.maximum(state[n][0], tile_max)
            weights = jnp.exp2((scores - peak) * EXP2_SCALE)
            total = jnp.sum(weights, axis=0, keepdims=True)
            mixed = mixing((hashes[n] + base) + k_iota)
            keeper = lax.shift_right_logical(mixed, jnp.int32(8)) >= 1677722
            dropped = jnp.where(keeper, weights, jnp.float32(0.0)).astype(jnp.bfloat16)
            value = jnp.dot(v_tile, dropped, preferred_element_type=jnp.float32)
            if not diagonal:
                rescale = jnp.exp2((state[n][0] - peak) * EXP2_SCALE)
                total = state[n][1] * rescale + total
                value = state[n][2] * rescale + value
            result.append((peak, total, value))
        return tuple(result)

    state = tile(block, None, True)
    state = lax.fori_loop(first_tile, block, lambda i, s: tile(i, s, False), state)
    for n in range(pair):
        _, total, value = state[n]
        value = value * (jnp.float32(1.0 / 0.9) / total)
        out_ref[:, n * HD : (n + 1) * HD] = value.T.astype(jnp.bfloat16)


def attend(queries, kv_all, doc_ids, drop_seed):
    rows, width = queries.shape
    local_heads = width // HD
    ctx_index = lax.axis_index("ctx").astype(jnp.int32)
    tp_index = lax.axis_index("tp").astype(jnp.int32)
    q_doc = lax.dynamic_slice_in_dim(doc_ids, ctx_index * rows, rows)
    doc_start = jnp.sum((doc_ids[:, None] < q_doc[None, :]).astype(jnp.int32), axis=0)
    meta = jnp.stack([doc_start[0] // rows, ctx_index, drop_seed[0], tp_index * local_heads])
    return pl.pallas_call(
        attend_kernel,
        grid_spec=pltpu.PrefetchScalarGridSpec(
            num_scalar_prefetch=1,
            grid=(local_heads // PAIR,),
            in_specs=[
                pl.BlockSpec((rows, PAIR * HD), lambda i, m: (0, i)),
                pl.BlockSpec(kv_all.shape, lambda i, m: (0, 0, 0, 0)),
                pl.BlockSpec((1, rows), lambda i, m: (0, 0)),
            ],
            out_specs=pl.BlockSpec((rows, PAIR * HD), lambda i, m: (0, i)),
        ),
        out_shape=jax.ShapeDtypeStruct(queries.shape, jnp.bfloat16),
        compiler_params=pltpu.CompilerParams(vmem_limit_bytes=48 * 1024 * 1024),
    )(meta, queries, kv_all, doc_start.reshape(1, rows))


def pack_kv(key_proj, value_proj):
    rows = key_proj.shape[0]
    local_kv = key_proj.shape[1] // HD
    keys = key_proj.reshape(rows, local_kv, HD).transpose(1, 0, 2)
    values = value_proj.reshape(rows // HD, HD, local_kv, HD).transpose(2, 0, 3, 1)
    return jnp.concatenate([keys, values.reshape(local_kv, rows, HD)], axis=1)


def project_kernel(size, subs, att_ref, weight_ref, out_ref, own, from_left, from_right, w_buf, w_sem, send_r, recv_r, send_l, recv_l):
    me = lax.axis_index("tp")
    width = w_buf.shape[2]
    tiles = size * subs
    slots = w_buf.shape[0]
    upper = (2 * me) // size

    def target(i):
        k = i // subs
        a = (k // 2) * (1 - k % 2) + (size - 1 - k // 2) * (k % 2)
        return a * upper + (size - 1 - a) * (1 - upper)

    def weight_copy(i):
        column = pl.multiple_of((target(i) * subs + i % subs) * width, width)
        return pltpu.make_async_copy(
            weight_ref.at[:, pl.ds(column, width)], w_buf.at[i % slots], w_sem.at[i % slots]
        )

    def right_copy(t, s):
        return pltpu.make_async_remote_copy(
            src_ref=own.at[t, s], dst_ref=from_left.at[t, s], send_sem=send_r.at[t, s],
            recv_sem=recv_r.at[t, s], device_id={"tp": lax.rem(me + 1, size)},
            device_id_type=pl.DeviceIdType.MESH,
        )

    def left_copy(t, s):
        return pltpu.make_async_remote_copy(
            src_ref=own.at[t, s], dst_ref=from_right.at[t, s], send_sem=send_l.at[t, s],
            recv_sem=recv_l.at[t, s], device_id={"tp": lax.rem(me + size - 1, size)},
            device_id_type=pl.DeviceIdType.MESH,
        )

    for i in range(slots - 1):
        weight_copy(i).start()
    barrier = pltpu.get_barrier_semaphore()

    @pl.when(me > 0)
    def _():
        pl.semaphore_signal(barrier, inc=1, device_id={"tp": me - 1}, device_id_type=pl.DeviceIdType.MESH)

    @pl.when(me < size - 1)
    def _():
        pl.semaphore_signal(barrier, inc=1, device_id={"tp": me + 1}, device_id_type=pl.DeviceIdType.MESH)

    @pl.when((me > 0) & (me < size - 1))
    def _():
        pl.semaphore_wait(barrier, 2)

    @pl.when((me == 0) | (me == size - 1))
    def _():
        pl.semaphore_wait(barrier, 1)

    def make_tile(i, carry):
        @pl.when(i + slots - 1 < tiles)
        def _():
            weight_copy(i + slots - 1).start()

        weight_copy(i).wait()
        t, s = target(i), i % subs
        own[t, s] = jnp.dot(
            att_ref[...], w_buf[i % slots], preferred_element_type=jnp.float32
        ).astype(jnp.bfloat16)

        @pl.when((me == 0) & (t > 0))
        def _():
            right_copy(t, s).start()

        @pl.when((me == size - 1) & (t < size - 1))
        def _():
            left_copy(t, s).start()

        return carry

    lax.fori_loop(0, tiles, make_tile, 0)

    def add(ref, t, s):
        total = own[t, s].astype(jnp.float32) + ref[t, s].astype(jnp.float32)
        own[t, s] = total.astype(jnp.bfloat16)

    def hand_on(i, carry):
        s = i % subs
        right_t = size - 1 - i // subs
        left_t = i // subs

        @pl.when((me > 0) & (right_t > me))
        def _():
            right_copy(right_t, s).wait_recv()
            add(from_left, right_t, s)
            right_copy(right_t, s).start()

        @pl.when((me < size - 1) & (left_t < me))
        def _():
            left_copy(left_t, s).wait_recv()
            add(from_right, left_t, s)
            left_copy(left_t, s).start()

        return carry

    lax.fori_loop(0, tiles, hand_on, 0)

    for s in range(subs):
        columns = slice(s * width, (s + 1) * width)

        @pl.when(me == 0)
        def _():
            left_copy(me, s).wait_recv()
            out_ref[:, columns] = (
                own[me, s].astype(jnp.float32) + from_right[me, s].astype(jnp.float32)
            ).astype(jnp.bfloat16)

        @pl.when(me == size - 1)
        def _():
            right_copy(me, s).wait_recv()
            out_ref[:, columns] = (
                own[me, s].astype(jnp.float32) + from_left[me, s].astype(jnp.float32)
            ).astype(jnp.bfloat16)

        @pl.when((me > 0) & (me < size - 1))
        def _():
            right_copy(me, s).wait_recv()
            left_copy(me, s).wait_recv()
            out_ref[:, columns] = (
                own[me, s].astype(jnp.float32)
                + from_left[me, s].astype(jnp.float32)
                + from_right[me, s].astype(jnp.float32)
            ).astype(jnp.bfloat16)

    def drain(i, carry):
        t, s = i // subs, i % subs

        @pl.when(t > me)
        def _():
            right_copy(t, s).wait_send()

        @pl.when(t < me)
        def _():
            left_copy(t, s).wait_send()

        return carry

    lax.fori_loop(0, tiles, drain, 0)


def project(attention, out_weight, size):
    rows, features = attention.shape
    columns = out_weight.shape[1] // size
    width = min(512, columns)
    subs = columns // width
    block = pltpu.VMEM((size, subs, rows, width), jnp.bfloat16)
    sems = pltpu.SemaphoreType.DMA((size, subs))
    return pl.pallas_call(
        functools.partial(project_kernel, size, subs),
        out_shape=jax.ShapeDtypeStruct((rows, columns), jnp.bfloat16),
        in_specs=[pl.BlockSpec(memory_space=pltpu.VMEM), pl.BlockSpec(memory_space=pl.ANY)],
        out_specs=pl.BlockSpec(memory_space=pltpu.VMEM),
        scratch_shapes=[
            block, block, block,
            pltpu.VMEM((3, features, width), jnp.bfloat16),
            pltpu.SemaphoreType.DMA((3,)),
            sems, sems, sems, sems,
        ],
        compiler_params=pltpu.CompilerParams(
            collective_id=0, has_side_effects=True, vmem_limit_bytes=48 * 1024 * 1024
        ),
    )(attention, out_weight)


def body(size, queries, key_proj, value_proj, out_weight, doc_ids, drop_seed):
    kv_all = lax.all_gather(pack_kv(key_proj, value_proj), "ctx", axis=0)
    attention = attend(queries, kv_all, doc_ids, drop_seed)
    return project(attention, out_weight, size)


def solution(mesh):
    in_specs = (P("ctx", "tp"), P("ctx", "tp"), P("ctx", "tp"), P("tp", None), P(), P())
    out_specs = P("ctx", "tp")
    return jax.shard_map(
        functools.partial(body, mesh.shape["tp"]), mesh=mesh, in_specs=in_specs, out_specs=out_specs, check_vma=False
    )
```
